128 devices in a mesh: azi: 32 (over z, y, core), ax: 4 (over x).
Axes of the slice: x: 4, y: 4, z: 4, core: 2. Of those that a mesh axis runs over, the one named last changes fastest.
Arguments:
- surface_data: bfloat16 [1024, 64, 2, 512], P('azi', 'ax'), may hold values from -6 to 6
- panel_pos: bfloat16 [3, 1024, 64], P(None, 'azi', 'ax'), may hold values from -0.3984375 to 0.3984375
- panel_normal: bfloat16 [3, 1024, 64], P(None, 'azi', 'ax'), may hold values from -3 to 3
- panel_area: bfloat16 [1024, 64], P('azi', 'ax'), may hold values from 0.099609375 to 1
- obs_pos: float32 [3, 98304], P(None, ('azi', 'ax')), may hold values from -0.4 to 0.4
- obs_angles: float32 [2, 768], P(None, ('azi', 'ax')), may hold values from -3.140625 to 3.140625
- send_list: int32 [128, 128], P(('azi', 'ax')), may hold values from -1 to 3, as said below
- entry_source: int32 [768, 32], P(('azi', 'ax')), may hold values from -1 to 127, as said below
- entry_offset: int32 [768, 32], P(('azi', 'ax')), may hold values from 16 to 252
Outputs:
- obs_pressure: float32 [98304, 256], P(('azi', 'ax'))
The draws below stay inside these ranges and needn't reach their ends.
Inputs may be any that keep to these rules, and one draw needn't show every extreme that they name: `send_list`: entry (s, r) is set to a block of device s exactly where some observer block of device r lists s in entry_source, and is -1 elsewhere. `entry_source`: each row lists distinct devices, its live entries first and -1 after them; some row has all 32 entries live.
All inputs are finite; a program needn't handle non-finite values.
Results may differ from the reference program's by a relative error of at most 0.0033.
Values may be sent and summed in bfloat16 or wider, within the bound.
A program may use at most 256 MiB of HBM per device.

```python
import math
import jax
import jax.numpy as jnp
from jax import lax

BLOCK = 128
BUF = 512
WIN = 256
AXL = 16
AZL = 32
OBLK_DEV = 6
KMAX = 32
BLOCKS_DEV = 4
NAZ = 1024
NAX = 64
NDEV = 128
OBLOCKS = 768
OBSERVERS = 98304
N_AZI = 32
N_AX = 4


def route_tables(key):
    subkeys = jax.random.split(jax.random.fold_in(key, 4099), 6)
    devices = N_AZI * N_AX
    block_total = OBLOCKS
    first_draw = jax.random.randint(subkeys[0], (block_total,), 0, KMAX - 3)
    second_draw = jax.random.randint(subkeys[1], (block_total,), 0, KMAX - 3)
    live_counts = 4 + first_draw * second_draw // KMAX
    fullest = jax.random.randint(subkeys[2], (), 0, block_total)
    positions = jnp.arange(block_total, dtype=jnp.int32)
    live_counts = jnp.where(positions == fullest, KMAX, live_counts)
    orders = jax.vmap(lambda sub_key: jax.random.permutation(sub_key, devices)[:KMAX])(jax.random.split(subkeys[3], block_total))
    columns = jnp.arange(KMAX, dtype=jnp.int32)
    sources = jnp.where(columns[None, :] < live_counts[:, None], orders, -1).astype(jnp.int32)
    owners = positions // OBLK_DEV
    used_pairs = jnp.zeros((devices, devices), jnp.int32).at[jnp.broadcast_to(owners[:, None], sources.shape), jnp.clip(sources, 0, devices - 1)].max((sources >= 0).astype(jnp.int32))
    picked = jax.random.randint(subkeys[4], (devices, devices), 0, BLOCKS_DEV)
    send_table = jnp.where(used_pairs.T > 0, picked, -1).astype(jnp.int32)
    offsets = jax.random.randint(subkeys[5], (block_total, KMAX), 16, BUF - WIN - 3)
    offsets = offsets.at[fullest, 0].set(BUF - WIN - 4).at[fullest, 1].set(16).astype(jnp.int32)
    return (send_table, sources, offsets)


def draw_send_list(key, part):
    return route_tables(key)[0]


def draw_entry_source(key, part):
    return route_tables(key)[1]


def draw_entry_offset(key, part):
    return route_tables(key)[2]


def steps_of(own_key, dims, pieces, low, largest):
    level, own = 1.0, jax.random.fold_in(own_key, 6)
    for position, shards_of in pieces:
        steps = jnp.exp(jax.random.uniform(jax.random.fold_in(own, position), (shards_of,), jnp.float32, low / len(pieces), largest / len(pieces)))
        level = level * jnp.repeat(steps, dims[position] // shards_of).reshape([-1 if axis == position else 1 for axis in range(len(dims))])
    return level


def gaussian(stream_key, extent, width, bound, cuts=(), kind=jnp.bfloat16):
    gain = steps_of(stream_key, extent, cuts, -0.22, 0.18) if cuts else 1.0
    result = jax.random.normal(stream_key, extent, jnp.float32) * width * gain
    return jnp.minimum(jnp.maximum(result, -bound), bound).astype(kind)


def setup_inputs(seed: int = 0) -> dict:
    key_of = jax.random.split(jax.random.key(seed), 10)
    return {
        "surface_data": gaussian(key_of[0], (NAZ, NAX, 2, BUF), 1.0, 6.0, ((0, 32), (1, 4))),
        "panel_pos": jnp.clip(jax.random.uniform(key_of[1], (3, NAZ, NAX), jnp.float32, -0.3984375, 0.3984375) * steps_of(key_of[1], (3, NAZ, NAX), ((1, 32), (2, 4)), -0.4, 0.0), -0.3984375, 0.3984375).astype(jnp.bfloat16),
        "panel_normal": gaussian(key_of[2], (3, NAZ, NAX), 0.5, 3.0, ((1, 32), (2, 4))),
        "panel_area": jnp.clip(jnp.exp(math.log(1.0) - 2.306499 * jax.random.uniform(key_of[3], (NAZ, NAX), jnp.float32) ** steps_of(key_of[3], (NAZ, NAX), ((0, 32), (1, 4)), -0.2, 0.2)), 0.099609375, 1.0).astype(jnp.bfloat16),
        "obs_pos": jnp.clip(jax.random.uniform(key_of[4], (3, OBSERVERS), jnp.float32, -0.4, 0.4) * steps_of(key_of[4], (3, OBSERVERS), ((1, 128),), -0.4, 0.0), -0.4, 0.4),
        "obs_angles": jnp.clip(jax.random.uniform(key_of[5], (2, OBLOCKS), jnp.float32, -3.140625, 3.140625), -3.140625, 3.140625),
        "send_list": draw_send_list(jax.random.fold_in(key_of[9], 71), 0),
        "entry_source": draw_entry_source(jax.random.fold_in(key_of[9], 71), 0),
        "entry_offset": draw_entry_offset(jax.random.fold_in(key_of[9], 71), 0),
    }


FOUR_PI = 4.0 * math.pi


def lagrange_taps(fraction):
    return jnp.stack([
        -(fraction - 1.0) * (fraction - 2.0) * (fraction - 3.0) / 6.0,
        fraction * (fraction - 2.0) * (fraction - 3.0) / 2.0,
        -fraction * (fraction - 1.0) * (fraction - 3.0) / 2.0,
        fraction * (fraction - 1.0) * (fraction - 2.0) / 6.0], 0)


def entry_term(signal, geometry, observer, angles, offset):
    sample_count = signal.shape[2] - 5
    widened = signal.astype(jnp.float32)
    slopes = (0.5 * (widened[:, :, 2:] - widened[:, :, :-2])).astype(jnp.bfloat16)
    levels_cut = signal[:, :, 1:-1]
    sources = jnp.stack([slopes[:, 1], levels_cut[:, 0], slopes[:, 0]], 0)
    shifted = jnp.stack([sources[:, :, lag_index:lag_index + sample_count] for lag_index in range(4)], 1)
    columns = shifted.reshape(-1, sample_count)
    direction = jnp.stack([jnp.cos(angles[0]) * jnp.cos(angles[1]), jnp.sin(angles[0]) * jnp.cos(angles[1]), jnp.sin(angles[1])])
    geometry_f = geometry.astype(jnp.float32)
    toward_obs = jnp.sum(direction[:, None] * observer, 0)
    toward_pan = jnp.sum(direction[:, None] * geometry_f[0:3], 0)
    facing = jnp.sum(direction[:, None] * geometry_f[3:6], 0)
    fraction = 1.5 + toward_obs[:, None] - toward_pan[None, :]
    inverse = 16.0 / (offset.astype(jnp.float32) + fraction)
    amplitudes = jnp.stack([geometry_f[6][None, :] * inverse, facing[None, :] * inverse, facing[None, :] * inverse * inverse], 0)
    tap_weights = lagrange_taps(fraction)
    weights = amplitudes[:, None] * tap_weights[None] / FOUR_PI
    matrix = jnp.transpose(weights, (2, 0, 1, 3)).reshape(fraction.shape[0], -1).astype(jnp.bfloat16)
    return jnp.dot(matrix, columns, preferred_element_type=jnp.float32)


def reference(surface_data, panel_pos, panel_normal, panel_area, obs_pos, obs_angles, send_list, entry_source, entry_offset):
    widened = surface_data.astype(jnp.float32)
    azimuth_pass = 0.25 * (jnp.roll(widened, 1, 0) + 2.0 * widened + jnp.roll(widened, -1, 0))
    framed = jnp.pad(azimuth_pass, ((0, 0), (1, 1), (0, 0), (0, 0)))
    filtered = (0.25 * (framed[:, :-2] + 2.0 * framed[:, 1:-1] + framed[:, 2:])).astype(jnp.bfloat16)
    geometry = jnp.concatenate([panel_pos, panel_normal, panel_area[None]], 0)
    band_rows = BLOCK // AXL
    empty_sum = jnp.zeros((BLOCK, WIN), jnp.float32)

    def per_block(block_items):
        block_id, sources, offsets = block_items
        owner_device = block_id // OBLK_DEV
        observer = lax.dynamic_slice(obs_pos, (jnp.int32(0), block_id * BLOCK), (3, BLOCK))
        angles = lax.dynamic_slice(obs_angles, (jnp.int32(0), block_id), (2, 1))[:, 0]

        def add_entry(running, pair):
            source, offset = pair
            slot_index = jnp.clip(source, 0, NDEV - 1).astype(jnp.int32)
            local_block = send_list[slot_index, owner_device]
            usable = (source >= 0) & (local_block >= 0)
            first_row = ((slot_index // N_AX) * AZL + jnp.clip(local_block, 0, BLOCKS_DEV - 1) * band_rows).astype(jnp.int32)
            first_col = ((slot_index % N_AX) * AXL).astype(jnp.int32)

            def compute(current):
                signal = lax.dynamic_slice(filtered, (first_row, first_col, jnp.int32(0), (offset - 1).astype(jnp.int32)), (band_rows, AXL, 2, WIN + 5)).reshape(BLOCK, 2, WIN + 5)
                geom_block = lax.dynamic_slice(geometry, (jnp.int32(0), first_row, first_col), (7, band_rows, AXL)).reshape(7, BLOCK)
                return current + entry_term(signal, geom_block, observer, angles, offset)

            return lax.cond(usable, compute, lambda current: current, running), None

        summed, _ = lax.scan(add_entry, empty_sum, (sources, offsets))
        return summed

    totals = lax.map(per_block, (jnp.arange(OBLOCKS, dtype=jnp.int32), entry_source, entry_offset))
    return totals.reshape(OBSERVERS, WIN)
```

```python
import math

import jax
import jax.numpy as jnp
from jax import lax
from jax.experimental import pallas as pl
from jax.experimental.pallas import tpu as pltpu
from jax.sharding import Mesh
from jax.sharding import PartitionSpec as P

BLOCK = 128
WIN = 256
BUF = 512
BLOCKS_HERE = 4
OWN = 6
NZ, NY, NC, NX = 4, 4, 2, 4
LINES = NZ * NY
GROUP = NC * NX
SLOTS = GROUP * BLOCKS_HERE
ROWS = LINES * OWN
SPAN = 272
PADDED = 528
FOUR_PI = 4.0 * math.pi
AZI = ("z", "y", "core")


def filter_local(surface_data):
    count = lax.axis_size("ax")
    up = [(i, i + 1) for i in range(count - 1)]
    down = [(b, a) for a, b in up]
    low = lax.ppermute(surface_data[:, -1:], "ax", up)
    high = lax.ppermute(surface_data[:, :1], "ax", down)
    framed = jnp.concatenate([low, surface_data, high], axis=1)
    count = NZ * NY * NC
    ring = [(i, (i + 1) % count) for i in range(count)]
    back = [(b, a) for a, b in ring]
    low = lax.ppermute(framed[-1:], AZI, ring)
    high = lax.ppermute(framed[:1], AZI, back)
    widened = jnp.concatenate([low, framed, high], axis=0).astype(jnp.float32)
    passed = 0.25 * (widened[:-2] + 2.0 * widened[1:-1] + widened[2:])
    filtered = 0.25 * (passed[:, :-2] + 2.0 * passed[:, 1:-1] + passed[:, 2:])
    return filtered.astype(jnp.bfloat16)


def entry_codes(sources, offsets, table, line):
    units = jnp.arange(GROUP, dtype=jnp.int32)
    wanted = line * GROUP + units
    match = sources[:, None, :] == wanted[None, :, None]
    offset = jnp.max(jnp.where(match, offsets[:, None, :], -1), axis=2)
    block = jnp.repeat(table.T, OWN, axis=0)
    live = (offset >= 0) & (block >= 0)
    code = offset * SLOTS + units[None, :] * BLOCKS_HERE + block
    place = jnp.cumsum(live.astype(jnp.int32), axis=1) - 1
    hit = live[:, :, None] & (place[:, :, None] == units[None, None, :])
    packed = jnp.sum(jnp.where(hit, code[:, :, None], 0), axis=1)
    return packed, jnp.sum(live.astype(jnp.int32), axis=1)


def partial_kernel(codes, counts, dirs, toward, geometry, signals, out, source, weights, total, reach_obs):
    def build(slot, carry):
        level = signals[slot].astype(jnp.float32)
        slope = 0.5 * (pltpu.roll(level, BUF - 1, 0) - pltpu.roll(level, 1, 0))
        slope = slope.astype(jnp.bfloat16).astype(jnp.float32)
        source[slot * 3, 0:BUF, :] = slope[:, 128:256]
        source[slot * 3 + 1, 0:BUF, :] = level[:, 0:128]
        source[slot * 3 + 2, 0:BUF, :] = slope[:, 0:128]
        for kind in range(3):
            source[slot * 3 + kind, BUF:PADDED, :] = jnp.zeros((PADDED - BUF, 128), jnp.float32)
        return carry

    lax.fori_loop(0, SLOTS, build, 0)

    def per_row(row, carry):
        d0, d1, d2 = dirs[row * 3], dirs[row * 3 + 1], dirs[row * 3 + 2]
        total[...] = jnp.zeros_like(total)
        line = jnp.broadcast_to(toward[pl.ds(row, 1), :], (BLOCK, BLOCK))
        reach_obs[...] = 1.5 + line.T

        def per_entry(position, inner):
            code = codes[row * GROUP + position]
            slot = lax.rem(code, SLOTS)
            offset = lax.div(code, SLOTS)
            offset_f = offset.astype(jnp.float32)
            geo = geometry[slot]
            toward_pan = d0 * geo[0:1] + d1 * geo[1:2] + d2 * geo[2:3]
            facing = (d0 * geo[3:4] + d1 * geo[4:5] + d2 * geo[5:6]) * (1.0 / FOUR_PI)
            area = geo[6:7] * (1.0 / FOUR_PI)
            for chunk in range(BLOCK // 16):
                fraction = reach_obs[chunk * 16 : chunk * 16 + 16, :] - toward_pan
                inverse = 16.0 / (offset_f + fraction)
                strength = facing * inverse
                amplitudes = (area * inverse, strength, strength * inverse)
                f1, f2, f3 = fraction - 1.0, fraction - 2.0, fraction - 3.0
                front, rear = fraction * f1, f2 * f3
                taps = (
                    f1 * rear * (-1.0 / 6.0),
                    fraction * rear * 0.5,
                    front * f3 * -0.5,
                    front * f2 * (1.0 / 6.0),
                )
                for tap_index in range(4):
                    pair, parity = divmod(tap_index, 2)
                    for kind in range(3):
                        column = (pair * 3 + kind) * 128
                        weights[
                            parity * 128 + chunk * 16 : parity * 128 + chunk * 16 + 16, column : column + 128
                        ] = (amplitudes[kind] * taps[tap_index]).astype(jnp.bfloat16)
            columns = jnp.concatenate(
                [
                    source[slot * 3 + kind, pl.ds(offset + 2 * pair, SPAN), :].astype(jnp.bfloat16)
                    for pair in range(2)
                    for kind in range(3)
                ],
                axis=1,
            )
            total[...] += lax.dot_general(
                columns, weights[...], (((1,), (1,)), ((), ())), preferred_element_type=jnp.float32
            )
            return inner

        lax.fori_loop(0, counts[row], per_entry, 0)
        out[row] = (total[0:WIN, 0:128] + total[1 : WIN + 1, 128:256]).astype(jnp.bfloat16)
        return carry

    lax.fori_loop(0, ROWS, per_row, 0)


def partial_sums(codes, counts, dirs, toward, geometry, signals, interpret=False):
    smem = pl.BlockSpec(memory_space=pltpu.SMEM)
    vmem = pl.BlockSpec(memory_space=pltpu.VMEM)
    return pl.pallas_call(
        partial_kernel,
        out_shape=jax.ShapeDtypeStruct((ROWS, WIN, BLOCK), jnp.bfloat16),
        in_specs=[smem, smem, smem, vmem, vmem, vmem],
        out_specs=vmem,
        scratch_shapes=[
            pltpu.VMEM((SLOTS * 3, PADDED, 128), jnp.float32),
            pltpu.VMEM((256, 768), jnp.bfloat16),
            pltpu.VMEM((SPAN, 256), jnp.float32),
            pltpu.VMEM((BLOCK, BLOCK), jnp.float32),
        ],
        compiler_params=pltpu.CompilerParams(vmem_limit_bytes=60 * 1024 * 1024),
        interpret=interpret,
    )(codes, counts, dirs, toward, geometry, signals)


def directions(angles):
    u, v = angles[..., 0], angles[..., 1]
    return jnp.stack([jnp.cos(u) * jnp.cos(v), jnp.sin(u) * jnp.cos(v), jnp.sin(v)], -1)


def body(
    surface_data,
    panel_pos,
    panel_normal,
    panel_area,
    obs_pos,
    obs_angles,
    send_list,
    entry_source,
    entry_offset,
):
    z, y = lax.axis_index("z"), lax.axis_index("y")
    core, ax = lax.axis_index("core"), lax.axis_index("ax")
    line = z * NY + y

    asked = jnp.concatenate(
        [
            obs_pos.reshape(-1),
            obs_angles.T.reshape(-1),
            entry_source.astype(jnp.float32).reshape(-1),
            entry_offset.astype(jnp.float32).reshape(-1),
        ]
    )
    asked = lax.all_gather(asked, ("z", "y"))
    n_pos, n_ang, n_ent = 3 * OWN * BLOCK, 2 * OWN, OWN * 32
    pos = asked[:, :n_pos].reshape(LINES, 3, OWN, BLOCK).transpose(0, 2, 1, 3).reshape(ROWS, 3, BLOCK)
    dirs = directions(asked[:, n_pos : n_pos + n_ang].reshape(ROWS, 2))
    entries = asked[:, n_pos + n_ang :].astype(jnp.int32)
    sources = entries[:, :n_ent].reshape(ROWS, 32)
    offsets = entries[:, n_ent:].reshape(ROWS, 32)
    toward = jnp.sum(dirs[:, :, None] * pos, axis=1)

    filtered = filter_local(surface_data)
    panels = filtered.reshape(BLOCKS_HERE, BLOCK, 2, BUF).transpose(0, 3, 2, 1).reshape(-1, 2 * BLOCK)
    geometry = jnp.concatenate(
        [panel_pos, panel_normal, panel_area[None], jnp.zeros_like(panel_area)[None]], 0
    ).reshape(8, BLOCKS_HERE, BLOCK).transpose(1, 0, 2)
    listed = send_list.astype(jnp.bfloat16)
    small = jnp.concatenate([geometry.reshape(-1), listed.reshape(-1), jnp.zeros((128,), jnp.bfloat16)])
    small_rows = small.shape[0] // 256
    small = jnp.pad(small.reshape(small_rows, 256), ((0, 32 - small_rows), (0, 0)))
    gathered = lax.all_gather(jnp.concatenate([panels, small], 0), ("core", "ax"))
    signals = gathered[:, : BLOCKS_HERE * BUF].reshape(SLOTS, BUF, 2 * BLOCK)
    small = gathered[:, BLOCKS_HERE * BUF :].reshape(GROUP, -1)
    geometry = small[:, : BLOCKS_HERE * 8 * BLOCK].reshape(SLOTS, 8, BLOCK).astype(jnp.float32)
    listed = small[:, BLOCKS_HERE * 8 * BLOCK : BLOCKS_HERE * 8 * BLOCK + 128].astype(jnp.int32)
    table = listed.reshape(GROUP, LINES, NC, NX)
    table = lax.dynamic_slice(table, (0, 0, core, ax), (GROUP, LINES, 1, 1)).reshape(GROUP, LINES)

    packed, counts = entry_codes(sources, offsets, table, line)
    sums = partial_sums(packed.reshape(-1), counts, dirs.reshape(-1), toward, geometry, signals)

    sums = sums.reshape(NZ, NY, OWN, WIN, BLOCK)
    sums = lax.all_to_all(sums, "y", split_axis=1, concat_axis=1, tiled=True)
    sums = jnp.sum(sums.astype(jnp.float32), axis=1).astype(jnp.bfloat16)
    sums = lax.all_to_all(sums, "z", split_axis=0, concat_axis=0, tiled=True)
    sums = jnp.sum(sums.astype(jnp.float32), axis=0)
    return sums.transpose(0, 2, 1).reshape(OWN * BLOCK, WIN)


def solution(mesh):
    split = Mesh(mesh.devices.reshape(NZ, NY, NC, NX), ("z", "y", "core", "ax"))
    azi, every = AZI, AZI + ("ax",)
    in_specs = (
        P(azi, "ax", None, None),
        P(None, azi, "ax"),
        P(None, azi, "ax"),
        P(azi, "ax"),
        P(None, every),
        P(None, every),
        P(every, None),
        P(every, None),
        P(every, None),
    )
    return jax.shard_map(body, mesh=split, in_specs=in_specs, out_specs=P(every, None), check_vma=False)
```

```python
import math

import jax
import jax.numpy as jnp
from jax import lax
from jax.experimental import pallas as pl
from jax.experimental.pallas import tpu as pltpu
from jax.sharding import Mesh
from jax.sharding import PartitionSpec as P

BLOCK = 128
WIN = 256
BUF = 512
BLOCKS_HERE = 4
OWN = 6
NZ, NY, NC, NX = 4, 4, 2, 4
LINES = NZ * NY
GROUP = NC * NX
SLOTS = GROUP * BLOCKS_HERE
ROWS = LINES * OWN
SPAN = 272
PADDED = 528
FOUR_PI = 4.0 * math.pi
AZI = ("z", "y", "core")
MESH = pl.DeviceIdType.MESH


def filter_local(surface_data):
    count = lax.axis_size("ax")
    up = [(i, i + 1) for i in range(count - 1)]
    down = [(b, a) for a, b in up]
    low = lax.ppermute(surface_data[:, -1:], "ax", up)
    high = lax.ppermute(surface_data[:, :1], "ax", down)
    framed = jnp.concatenate([low, surface_data, high], axis=1)
    count = NZ * NY * NC
    ring = [(i, (i + 1) % count) for i in range(count)]
    back = [(b, a) for a, b in ring]
    low = lax.ppermute(framed[-1:], AZI, ring)
    high = lax.ppermute(framed[:1], AZI, back)
    widened = jnp.concatenate([low, framed, high], axis=0).astype(jnp.float32)
    passed = 0.25 * (widened[:-2] + 2.0 * widened[1:-1] + widened[2:])
    filtered = 0.25 * (passed[:, :-2] + 2.0 * passed[:, 1:-1] + passed[:, 2:])
    return filtered.astype(jnp.bfloat16)


def entry_codes(sources, offsets, table, line):
    units = jnp.arange(GROUP, dtype=jnp.int32)
    wanted = line * GROUP + units
    match = sources[:, None, :] == wanted[None, :, None]
    offset = jnp.max(jnp.where(match, offsets[:, None, :], -1), axis=2)
    block = jnp.repeat(table.T, OWN, axis=0)
    live = (offset >= 0) & (block >= 0)
    code = offset * SLOTS + units[None, :] * BLOCKS_HERE + block
    place = jnp.cumsum(live.astype(jnp.int32), axis=1) - 1
    hit = live[:, :, None] & (place[:, :, None] == units[None, None, :])
    packed = jnp.sum(jnp.where(hit, code[:, :, None], 0), axis=1)
    return packed, jnp.sum(live.astype(jnp.int32), axis=1)


def partial_kernel(codes, counts, dirs, toward, geometry, signals, out, source, weights, total, reach_obs):
    def build(slot, carry):
        level = signals[slot].astype(jnp.float32)
        slope = 0.5 * (pltpu.roll(level, BUF - 1, 0) - pltpu.roll(level, 1, 0))
        slope = slope.astype(jnp.bfloat16).astype(jnp.float32)
        source[slot * 3, 0:BUF, :] = slope[:, 128:256]
        source[slot * 3 + 1, 0:BUF, :] = level[:, 0:128]
        source[slot * 3 + 2, 0:BUF, :] = slope[:, 0:128]
        for kind in range(3):
            source[slot * 3 + kind, BUF:PADDED, :] = jnp.zeros((PADDED - BUF, 128), jnp.float32)
        return carry

    lax.fori_loop(0, SLOTS, build, 0)

    def per_row(row, carry):
        d0, d1, d2 = dirs[row * 3], dirs[row * 3 + 1], dirs[row * 3 + 2]
        total[...] = jnp.zeros_like(total)
        line = jnp.broadcast_to(toward[pl.ds(row, 1), :], (BLOCK, BLOCK))
        reach_obs[...] = 1.5 + line.T

        def per_entry(position, inner):
            code = codes[row * GROUP + position]
            slot = lax.rem(code, SLOTS)
            offset = lax.div(code, SLOTS)
            offset_f = offset.astype(jnp.float32)
            geo = geometry[slot]
            toward_pan = d0 * geo[0:1] + d1 * geo[1:2] + d2 * geo[2:3]
            facing = (d0 * geo[3:4] + d1 * geo[4:5] + d2 * geo[5:6]) * (1.0 / FOUR_PI)
            area = geo[6:7] * (1.0 / FOUR_PI)
            for chunk in range(BLOCK // 16):
                fraction = reach_obs[chunk * 16 : chunk * 16 + 16, :] - toward_pan
                inverse = 16.0 / (offset_f + fraction)
                strength = facing * inverse
                amplitudes = (area * inverse, strength, strength * inverse)
                f1, f2, f3 = fraction - 1.0, fraction - 2.0, fraction - 3.0
                front, rear = fraction * f1, f2 * f3
                taps = (
                    f1 * rear * (-1.0 / 6.0),
                    fraction * rear * 0.5,
                    front * f3 * -0.5,
                    front * f2 * (1.0 / 6.0),
                )
                for tap_index in range(4):
                    pair, parity = divmod(tap_index, 2)
                    for kind in range(3):
                        column = (pair * 3 + kind) * 128
                        weights[
                            parity * 128 + chunk * 16 : parity * 128 + chunk * 16 + 16, column : column + 128
                        ] = (amplitudes[kind] * taps[tap_index]).astype(jnp.bfloat16)
            columns = jnp.concatenate(
                [
                    source[slot * 3 + kind, pl.ds(offset + 2 * pair, SPAN), :].astype(jnp.bfloat16)
                    for pair in range(2)
                    for kind in range(3)
                ],
                axis=1,
            )
            total[...] += lax.dot_general(
                columns, weights[...], (((1,), (1,)), ((), ())), preferred_element_type=jnp.float32
            )
            return inner

        lax.fori_loop(0, counts[row], per_entry, 0)
        out[0, row] = (total[0:128, 0:128] + total[1:129, 128:256]).astype(jnp.bfloat16)
        out[1, row] = (total[128:256, 0:128] + total[129:257, 128:256]).astype(jnp.bfloat16)
        return carry

    lax.fori_loop(0, ROWS, per_row, 0)


def partial_sums(codes, counts, dirs, toward, geometry, signals, interpret=False):
    smem = pl.BlockSpec(memory_space=pltpu.SMEM)
    vmem = pl.BlockSpec(memory_space=pltpu.VMEM)
    return pl.pallas_call(
        partial_kernel,
        out_shape=jax.ShapeDtypeStruct((2, ROWS, WIN // 2, BLOCK), jnp.bfloat16),
        in_specs=[smem, smem, smem, vmem, vmem, vmem],
        out_specs=vmem,
        scratch_shapes=[
            pltpu.VMEM((SLOTS * 3, PADDED, 128), jnp.float32),
            pltpu.VMEM((256, 768), jnp.bfloat16),
            pltpu.VMEM((SPAN, 256), jnp.float32),
            pltpu.VMEM((BLOCK, BLOCK), jnp.float32),
        ],
        compiler_params=pltpu.CompilerParams(vmem_limit_bytes=60 * 1024 * 1024),
        interpret=interpret,
    )(codes, counts, dirs, toward, geometry, signals)


def wrap(index):
    return lax.rem(index + 4, 4)


def reduce_kernel(sums, out, relay, message, forward, reduced, relay2, message2, forward2, send, recv):
    z, y = lax.axis_index("z"), lax.axis_index("y")
    axes = (("y", "z"), ("z", "y"))
    places = ((y, z), (z, y))
    barrier = pltpu.get_barrier_semaphore()
    for axis, place in (("y", y), ("z", z)):
        for step in (1, -1):
            pl.semaphore_signal(barrier, inc=1, device_id={axis: wrap(place + step)}, device_id_type=MESH)
    pl.semaphore_wait(barrier, 4)

    def piece(half, first, second):
        if half == 0:
            return sums.at[0, second, first]
        return sums.at[1, first, second]

    def copy(number, half, stage, step, src, dst):
        axis = axes[half][stage]
        return pltpu.make_async_remote_copy(
            src_ref=src,
            dst_ref=dst,
            send_sem=send.at[half, stage, number],
            recv_sem=recv.at[half, stage, number],
            device_id={axis: wrap(places[half][stage] + step)},
            device_id_type=MESH,
        )

    low, high = pl.ds(0, 2), pl.ds(2, 2)
    first_copies = []
    for half in range(2):
        me = places[half][0]
        there, after, before = wrap(me + 2), wrap(me + 1), wrap(me - 1)
        batch = [
            copy(0, half, 0, 1, piece(half, there, low), relay.at[half, 0]),
            copy(1, half, 0, -1, piece(half, there, high), relay.at[half, 1]),
            copy(2, half, 0, 1, piece(half, after, high), message.at[half, 0, high]),
            copy(3, half, 0, -1, piece(half, before, low), message.at[half, 1, low]),
        ]
        first_copies.append(batch)
    for number in range(4):
        for half in range(2):
            first_copies[half][number].start()

    for half in range(2):
        me = places[half][0]
        for side, step, offset in ((0, 1, 0), (1, -1, 2)):
            first_copies[half][side].wait_recv()

            def add_relay(index, carry, half=half, side=side, step=step, offset=offset, me=me):
                second, block = lax.div(index, OWN), lax.rem(index, OWN)
                own = piece(half, wrap(me + step), second + offset)[block]
                got = relay[half, side, second, block]
                forward[half, side, second, block] = (own.astype(jnp.float32) + got.astype(jnp.float32)).astype(
                    jnp.bfloat16
                )
                return carry

            lax.fori_loop(0, 2 * OWN, add_relay, 0)
            last = copy(4 + side, half, 0, step, forward.at[half, side], message.at[half, side, pl.ds(offset, 2)])
            last.start()
            first_copies[half].append(last)

    second_copies = [[], []]
    for half in range(2):
        for number in range(2, 6):
            first_copies[half][number].wait_recv()
        me, other = places[half]

        def add_first(index, carry, half=half, me=me):
            second, block = lax.div(index, OWN), lax.rem(index, OWN)
            value = piece(half, me, second)[block].astype(jnp.float32)
            value += message[half, 0, second, block].astype(jnp.float32)
            value += message[half, 1, second, block].astype(jnp.float32)
            reduced[half, second, block] = value.astype(jnp.bfloat16)
            return carry

        lax.fori_loop(0, 4 * OWN, add_first, 0)
        there, after, before = wrap(other + 2), wrap(other + 1), wrap(other - 1)
        low3, high3 = pl.ds(0, 3), pl.ds(3, 3)
        batch = [
            copy(0, half, 1, 1, reduced.at[half, there, low3], relay2.at[half, 0]),
            copy(1, half, 1, -1, reduced.at[half, there, high3], relay2.at[half, 1]),
            copy(2, half, 1, 1, reduced.at[half, after, high3], message2.at[half, 0, high3]),
            copy(3, half, 1, -1, reduced.at[half, before, low3], message2.at[half, 1, low3]),
        ]
        for item in batch:
            item.start()
        second_copies[half] = batch

    for half in range(2):
        other = places[half][1]
        for side, step, offset in ((0, 1, 0), (1, -1, 3)):
            second_copies[half][side].wait_recv()
            target = wrap(other + step)
            for block in range(3):
                own = reduced[half, target, block + offset].astype(jnp.float32)
                got = relay2[half, side, block].astype(jnp.float32)
                forward2[half, side, block] = (own + got).astype(jnp.bfloat16)
            last = copy(4 + side, half, 1, step, forward2.at[half, side], message2.at[half, side, pl.ds(offset, 3)])
            last.start()
            second_copies[half].append(last)

    for half in range(2):
        other = places[half][1]
        for number in range(2, 6):
            second_copies[half][number].wait_recv()
        for block in range(OWN):
            value = reduced[half, other, block].astype(jnp.float32)
            value += message2[half, 0, block].astype(jnp.float32)
            value += message2[half, 1, block].astype(jnp.float32)
            out[block * BLOCK : (block + 1) * BLOCK, half * 128 : half * 128 + 128] = value.T

    for half in range(2):
        for item in first_copies[half] + second_copies[half]:
            item.wait_send()


def owner_sums(sums):
    vmem = pl.BlockSpec(memory_space=pltpu.VMEM)
    tile = (WIN // 2, BLOCK)
    return pl.pallas_call(
        reduce_kernel,
        out_shape=jax.ShapeDtypeStruct((OWN * BLOCK, WIN), jnp.float32),
        in_specs=[vmem],
        out_specs=vmem,
        scratch_shapes=[
            pltpu.VMEM((2, 2, 2, OWN, *tile), jnp.bfloat16),
            pltpu.VMEM((2, 2, 4, OWN, *tile), jnp.bfloat16),
            pltpu.VMEM((2, 2, 2, OWN, *tile), jnp.bfloat16),
            pltpu.VMEM((2, 4, OWN, *tile), jnp.bfloat16),
            pltpu.VMEM((2, 2, 3, *tile), jnp.bfloat16),
            pltpu.VMEM((2, 2, OWN, *tile), jnp.bfloat16),
            pltpu.VMEM((2, 2, 3, *tile), jnp.bfloat16),
            pltpu.SemaphoreType.DMA((2, 2, 6)),
            pltpu.SemaphoreType.DMA((2, 2, 6)),
        ],
        compiler_params=pltpu.CompilerParams(
            collective_id=1, has_side_effects=True, vmem_limit_bytes=40 * 1024 * 1024
        ),
    )(sums)


def directions(angles):
    u, v = angles[..., 0], angles[..., 1]
    return jnp.stack([jnp.cos(u) * jnp.cos(v), jnp.sin(u) * jnp.cos(v), jnp.sin(v)], -1)


def body(
    surface_data,
    panel_pos,
    panel_normal,
    panel_area,
    obs_pos,
    obs_angles,
    send_list,
    entry_source,
    entry_offset,
):
    z, y = lax.axis_index("z"), lax.axis_index("y")
    core, ax = lax.axis_index("core"), lax.axis_index("ax")
    line = z * NY + y

    asked = jnp.concatenate(
        [
            obs_pos.reshape(-1),
            obs_angles.T.reshape(-1),
            entry_source.astype(jnp.float32).reshape(-1),
            entry_offset.astype(jnp.float32).reshape(-1),
        ]
    )
    asked = lax.all_gather(asked, ("z", "y"))
    n_pos, n_ang, n_ent = 3 * OWN * BLOCK, 2 * OWN, OWN * 32
    pos = asked[:, :n_pos].reshape(LINES, 3, OWN, BLOCK).transpose(0, 2, 1, 3).reshape(ROWS, 3, BLOCK)
    dirs = directions(asked[:, n_pos : n_pos + n_ang].reshape(ROWS, 2))
    entries = asked[:, n_pos + n_ang :].astype(jnp.int32)
    sources = entries[:, :n_ent].reshape(ROWS, 32)
    offsets = entries[:, n_ent:].reshape(ROWS, 32)
    toward = jnp.sum(dirs[:, :, None] * pos, axis=1)

    filtered = filter_local(surface_data)
    panels = filtered.reshape(BLOCKS_HERE, BLOCK, 2, BUF).transpose(0, 3, 2, 1).reshape(-1, 2 * BLOCK)
    geometry = jnp.concatenate(
        [panel_pos, panel_normal, panel_area[None], jnp.zeros_like(panel_area)[None]], 0
    ).reshape(8, BLOCKS_HERE, BLOCK).transpose(1, 0, 2)
    listed = send_list.astype(jnp.bfloat16)
    small = jnp.concatenate([geometry.reshape(-1), listed.reshape(-1), jnp.zeros((128,), jnp.bfloat16)])
    small_rows = small.shape[0] // 256
    small = jnp.pad(small.reshape(small_rows, 256), ((0, 32 - small_rows), (0, 0)))
    gathered = lax.all_gather(jnp.concatenate([panels, small], 0), ("core", "ax"))
    signals = gathered[:, : BLOCKS_HERE * BUF].reshape(SLOTS, BUF, 2 * BLOCK)
    small = gathered[:, BLOCKS_HERE * BUF :].reshape(GROUP, -1)
    geometry = small[:, : BLOCKS_HERE * 8 * BLOCK].reshape(SLOTS, 8, BLOCK).astype(jnp.float32)
    listed = small[:, BLOCKS_HERE * 8 * BLOCK : BLOCKS_HERE * 8 * BLOCK + 128].astype(jnp.int32)
    table = listed.reshape(GROUP, LINES, NC, NX)
    table = lax.dynamic_slice(table, (0, 0, core, ax), (GROUP, LINES, 1, 1)).reshape(GROUP, LINES)

    packed, counts = entry_codes(sources, offsets, table, line)
    sums = partial_sums(packed.reshape(-1), counts, dirs.reshape(-1), toward, geometry, signals)

    return owner_sums(sums.reshape(2, NZ, NY, OWN, WIN // 2, BLOCK))


def solution(mesh):
    split = Mesh(mesh.devices.reshape(NZ, NY, NC, NX), ("z", "y", "core", "ax"))
    azi, every = AZI, AZI + ("ax",)
    in_specs = (
        P(azi, "ax", None, None),
        P(None, azi, "ax"),
        P(None, azi, "ax"),
        P(azi, "ax"),
        P(None, every),
        P(None, every),
        P(every, None),
        P(every, None),
        P(every, None),
    )
    return jax.shard_map(body, mesh=split, in_specs=in_specs, out_specs=P(every, None), check_vma=False)
```

```python
import math

import jax
import jax.numpy as jnp
from jax import lax
from jax.experimental import pallas as pl
from jax.experimental.pallas import tpu as pltpu
from jax.sharding import Mesh
from jax.sharding import PartitionSpec as P

BLOCK = 128
WIN = 256
BUF = 512
BLOCKS_HERE = 4
AXL = 16
AZL = 32
OWN = 6
NZ, NY, NC, NX = 4, 4, 2, 4
LINES = NZ * NY
GROUP = NC * NX
SLOTS = GROUP * BLOCKS_HERE
ROWS = LINES * OWN
SPAN = 272
PADDED = 528
FOUR_PI = 4.0 * math.pi
AZI = ("z", "y", "core")
MESH = pl.DeviceIdType.MESH


def wrap(index):
    return lax.rem(index + 4, 4)


def gather_kernel(
    surface, edges, small, obs_pos, dirs, sources, offsets,
    signals, asked,
    own, own_asked, row_halo, col_halo, corners, edge_pass, smooth,
    send, recv, local,
):
    z, y = lax.axis_index("z"), lax.axis_index("y")
    core, ax = lax.axis_index("core"), lax.axis_index("ax")
    line = z * NY + y
    azimuth = line * NC + core
    unit = core * NX + ax

    def azi_device(index):
        index = lax.rem(index + NZ * NY * NC, NZ * NY * NC)
        return {"z": index // (NY * NC), "y": lax.rem(index // NC, NY), "core": lax.rem(index, NC)}

    following, preceding = azi_device(azimuth + 1), azi_device(azimuth - 1)
    right, left = {"ax": wrap(ax + 1)}, {"ax": wrap(ax - 1)}
    sibling = {"core": 1 - core}
    plane = [{"z": wrap(z + k // NY), "y": wrap(y + k % NY)} for k in range(1, LINES)]

    barrier = pltpu.get_barrier_semaphore()
    for device in [following, preceding, right, left] + plane:
        pl.semaphore_signal(barrier, inc=1, device_id=device, device_id_type=MESH)
    pl.semaphore_wait(barrier, 4 + len(plane))

    started = []

    def push(src, dst, device):
        number = len(started)
        item = pltpu.make_async_remote_copy(
            src_ref=src,
            dst_ref=dst,
            send_sem=send.at[number],
            recv_sem=recv.at[number],
            device_id=device,
            device_id_type=MESH,
        )
        item.start()
        started.append(item)
        return item

    col_low = push(edges.at[1], col_halo.at[0], right)
    col_high = push(edges.at[0], col_halo.at[1], left)
    row_low = push(surface.at[AZL - 1], row_halo.at[0], following)
    row_high = push(surface.at[0], row_halo.at[1], preceding)

    own_asked[...] = jnp.zeros_like(own_asked)
    for index in range(3 * OWN):
        part, block = divmod(index, OWN)
        own_asked[index : index + 1, :] = obs_pos[part : part + 1, block * BLOCK : (block + 1) * BLOCK]
    own_asked[24 : 24 + OWN, 0:32] = sources[...].astype(jnp.float32)
    own_asked[32 : 32 + OWN, 0:32] = offsets[...].astype(jnp.float32)
    own_asked[40:43, 0:OWN] = dirs[...]
    own[BLOCKS_HERE * BUF :, :] = small[...]

    col_low.wait_recv()
    col_high.wait_recv()
    corner_low = push(col_halo.at[:, pl.ds(16, 16)], corners.at[0], following)
    corner_high = push(col_halo.at[:, pl.ds(0, 16)], corners.at[1], preceding)
    row_low.wait_recv()
    row_high.wait_recv()
    corner_low.wait_recv()
    corner_high.wait_recv()
    tables = [push(own_asked, asked.at[line], device) for device in plane]
    keep_asked = pltpu.make_async_copy(own_asked, asked.at[line], local.at[4])
    keep_asked.start()

    row32 = lax.broadcasted_iota(jnp.int32, (AZL, 2 * BUF), 0)
    for side in range(2):
        mid = col_halo[side].astype(jnp.float32)
        above = jnp.where(row32 == 0, corners[0, side, 15:16, :].astype(jnp.float32), pltpu.roll(mid, 1, 0))
        below = jnp.where(row32 == AZL - 1, corners[1, side, 0:1, :].astype(jnp.float32), pltpu.roll(mid, AZL - 1, 0))
        there = (ax > 0) if side == 0 else (ax < NX - 1)
        edge_pass[side] = jnp.where(there, 0.25 * (above + 2.0 * mid + below), 0.0)

    chunks = [(0, BUF), (BUF, BUF), (2 * BUF, BUF), (3 * BUF, BUF + 32)]
    row16 = lax.broadcasted_iota(jnp.int32, (AXL, 2 * BUF), 0)
    to_right, to_left, to_sibling, kept = {}, {}, {}, []

    def region(owner_core, owner_ax, chunk):
        start, size = chunks[chunk]
        return signals.at[owner_core * NX + owner_ax, pl.ds(start, size)]

    def make_block(block):
        for part in range(8):
            row = block * 8 + part
            above = row_halo[0] if row == 0 else surface[row - 1]
            below = row_halo[1] if row == AZL - 1 else surface[row + 1]
            passed = 0.25 * (
                above.astype(jnp.float32) + 2.0 * surface[row].astype(jnp.float32) + below.astype(jnp.float32)
            )
            before = jnp.where(row16 == 0, edge_pass[0, row : row + 1, :], pltpu.roll(passed, 1, 0))
            after = jnp.where(row16 == AXL - 1, edge_pass[1, row : row + 1, :], pltpu.roll(passed, AXL - 1, 0))
            smooth[part * 16 : part * 16 + 16, :] = 0.25 * (before + 2.0 * passed + after)
        for channel in range(2):
            for part in range(4):
                tile = smooth[:, channel * BUF + part * 128 : channel * BUF + part * 128 + 128]
                own[
                    block * BUF + part * 128 : block * BUF + part * 128 + 128, channel * 128 : channel * 128 + 128
                ] = tile.T.astype(jnp.bfloat16)

    for chunk in range(4):
        make_block(chunk)
        start, size = chunks[chunk]
        mine = own.at[pl.ds(start, size)]
        to_right[chunk] = push(mine, region(core, ax, chunk), right)
        to_left[chunk] = push(mine, region(core, ax, chunk), left)
        to_sibling[chunk] = push(mine, region(core, ax, chunk), sibling)
        keep = pltpu.make_async_copy(mine, region(core, ax, chunk), local.at[chunk])
        keep.start()
        kept.append(keep)

    later = []
    for chunk in range(4):
        to_right[chunk].wait_recv()
        came = region(core, wrap(ax - 1), chunk)
        if chunk < 2:
            later.append((push(came, came, right), wrap(ax - 2), chunk))
        to_sibling[chunk + 10] = push(came, came, sibling)
        to_left[chunk].wait_recv()
        came = region(core, wrap(ax + 1), chunk)
        if chunk >= 2:
            later.append((push(came, came, left), wrap(ax + 2), chunk))
        to_sibling[chunk + 20] = push(came, came, sibling)
    for item, opposite, chunk in later:
        item.wait_recv()
        came = region(core, opposite, chunk)
        to_sibling[chunk + 30] = push(came, came, sibling)
    for item in to_sibling.values():
        item.wait_recv()
    for item in tables:
        item.wait_recv()
    keep_asked.wait()
    for item in kept:
        item.wait()
    for item in started:
        item.wait_send()


def gather(surface, edges, small, obs_pos, dirs, sources, offsets):
    vmem = pl.BlockSpec(memory_space=pltpu.VMEM)
    anywhere = pl.BlockSpec(memory_space=pl.ANY)
    copies = 6 + (LINES - 1) + 12 + 8 + 4 + 4
    rows = BLOCKS_HERE * BUF + 32
    return pl.pallas_call(
        gather_kernel,
        out_shape=(
            jax.ShapeDtypeStruct((GROUP, rows, 2 * BLOCK), jnp.bfloat16),
            jax.ShapeDtypeStruct((LINES, 48, 128), jnp.float32),
        ),
        in_specs=[vmem] * 7,
        out_specs=(anywhere, anywhere),
        scratch_shapes=[
            pltpu.VMEM((rows, 2 * BLOCK), jnp.bfloat16),
            pltpu.VMEM((48, 128), jnp.float32),
            pltpu.VMEM((2, AXL, 2 * BUF), jnp.bfloat16),
            pltpu.VMEM((2, AZL, 2 * BUF), jnp.bfloat16),
            pltpu.VMEM((2, 2, 16, 2 * BUF), jnp.bfloat16),
            pltpu.VMEM((2, AZL, 2 * BUF), jnp.float32),
            pltpu.VMEM((BLOCK, 2 * BUF), jnp.float32),
            pltpu.SemaphoreType.DMA((copies,)),
            pltpu.SemaphoreType.DMA((copies,)),
            pltpu.SemaphoreType.DMA((5,)),
        ],
        compiler_params=pltpu.CompilerParams(
            collective_id=2, has_side_effects=True, vmem_limit_bytes=40 * 1024 * 1024
        ),
    )(surface, edges, small, obs_pos, dirs, sources, offsets)


def entry_codes(sources, offsets, table, line):
    units = jnp.arange(GROUP, dtype=jnp.int32)
    wanted = line * GROUP + units
    match = sources[:, None, :] == wanted[None, :, None]
    offset = jnp.max(jnp.where(match, offsets[:, None, :], -1), axis=2)
    block = jnp.repeat(table.T, OWN, axis=0)
    live = (offset >= 0) & (block >= 0)
    code = offset * SLOTS + units[None, :] * BLOCKS_HERE + block
    place = jnp.cumsum(live.astype(jnp.int32), axis=1) - 1
    hit = live[:, :, None] & (place[:, :, None] == units[None, None, :])
    packed = jnp.sum(jnp.where(hit, code[:, :, None], 0), axis=1)
    return packed, jnp.sum(live.astype(jnp.int32), axis=1)


def partial_kernel(codes, counts, dirs, toward, geometry, signals, out, source, weights, total, reach_obs):
    def build(slot, carry):
        rows = pl.ds(pl.multiple_of(lax.rem(slot, BLOCKS_HERE) * BUF, BUF), BUF)
        level = signals[lax.div(slot, BLOCKS_HERE), rows, :].astype(jnp.float32)
        slope = 0.5 * (pltpu.roll(level, BUF - 1, 0) - pltpu.roll(level, 1, 0))
        slope = slope.astype(jnp.bfloat16).astype(jnp.float32)
        source[slot * 3, 0:BUF, :] = slope[:, 128:256]
        source[slot * 3 + 1, 0:BUF, :] = level[:, 0:128]
        source[slot * 3 + 2, 0:BUF, :] = slope[:, 0:128]
        for kind in range(3):
            source[slot * 3 + kind, BUF:PADDED, :] = jnp.zeros((PADDED - BUF, 128), jnp.float32)
        return carry

    lax.fori_loop(0, SLOTS, build, 0)

    def per_row(row, carry):
        d0, d1, d2 = dirs[row * 3], dirs[row * 3 + 1], dirs[row * 3 + 2]
        total[...] = jnp.zeros_like(total)
        line = jnp.broadcast_to(toward[pl.ds(row, 1), :], (BLOCK, BLOCK))
        reach_obs[...] = 1.5 + line.T

        def per_entry(position, inner):
            code = codes[row * GROUP + position]
            slot = lax.rem(code, SLOTS)
            offset = lax.div(code, SLOTS)
            offset_f = offset.astype(jnp.float32)
            geo = geometry[slot]
            toward_pan = d0 * geo[0:1] + d1 * geo[1:2] + d2 * geo[2:3]
            facing = (d0 * geo[3:4] + d1 * geo[4:5] + d2 * geo[5:6]) * (1.0 / FOUR_PI)
            area = geo[6:7] * (1.0 / FOUR_PI)
            for chunk in range(BLOCK // 16):
                fraction = reach_obs[chunk * 16 : chunk * 16 + 16, :] - toward_pan
                inverse = 16.0 / (offset_f + fraction)
                strength = facing * inverse
                amplitudes = (area * inverse, strength, strength * inverse)
                f1, f2, f3 = fraction - 1.0, fraction - 2.0, fraction - 3.0
                front, rear = fraction * f1, f2 * f3
                taps = (
                    f1 * rear * (-1.0 / 6.0),
                    fraction * rear * 0.5,
                    front * f3 * -0.5,
                    front * f2 * (1.0 / 6.0),
                )
                for tap_index in range(4):
                    pair, parity = divmod(tap_index, 2)
                    for kind in range(3):
                        column = (pair * 3 + kind) * 128
                        weights[
                            parity * 128 + chunk * 16 : parity * 128 + chunk * 16 + 16, column : column + 128
                        ] = (amplitudes[kind] * taps[tap_index]).astype(jnp.bfloat16)
            columns = jnp.concatenate(
                [
                    source[slot * 3 + kind, pl.ds(offset + 2 * pair, SPAN), :].astype(jnp.bfloat16)
                    for pair in range(2)
                    for kind in range(3)
                ],
                axis=1,
            )
            total[...] += lax.dot_general(
                columns, weights[...], (((1,), (1,)), ((), ())), preferred_element_type=jnp.float32
            )
            return inner

        lax.fori_loop(0, counts[row], per_entry, 0)
        out[0, row] = (total[0:128, 0:128] + total[1:129, 128:256]).astype(jnp.bfloat16)
        out[1, row] = (total[128:256, 0:128] + total[129:257, 128:256]).astype(jnp.bfloat16)
        return carry

    lax.fori_loop(0, ROWS, per_row, 0)


def partial_sums(codes, counts, dirs, toward, geometry, signals, interpret=False):
    smem = pl.BlockSpec(memory_space=pltpu.SMEM)
    vmem = pl.BlockSpec(memory_space=pltpu.VMEM)
    return pl.pallas_call(
        partial_kernel,
        out_shape=jax.ShapeDtypeStruct((2, ROWS, WIN // 2, BLOCK), jnp.bfloat16),
        in_specs=[smem, smem, smem, vmem, vmem, vmem],
        out_specs=vmem,
        scratch_shapes=[
            pltpu.VMEM((SLOTS * 3, PADDED, 128), jnp.float32),
            pltpu.VMEM((256, 768), jnp.bfloat16),
            pltpu.VMEM((SPAN, 256), jnp.float32),
            pltpu.VMEM((BLOCK, BLOCK), jnp.float32),
        ],
        compiler_params=pltpu.CompilerParams(vmem_limit_bytes=60 * 1024 * 1024),
        interpret=interpret,
    )(codes, counts, dirs, toward, geometry, signals)


def reduce_kernel(sums, out, relay, message, forward, reduced, relay2, message2, forward2, send, recv):
    z, y = lax.axis_index("z"), lax.axis_index("y")
    axes = (("y", "z"), ("z", "y"))
    places = ((y, z), (z, y))
    barrier = pltpu.get_barrier_semaphore()
    for axis, place in (("y", y), ("z", z)):
        for step in (1, -1):
            pl.semaphore_signal(barrier, inc=1, device_id={axis: wrap(place + step)}, device_id_type=MESH)
    pl.semaphore_wait(barrier, 4)

    def piece(half, first, second):
        if half == 0:
            return sums.at[0, second, first]
        return sums.at[1, first, second]

    def copy(number, half, stage, step, src, dst):
        axis = axes[half][stage]
        return pltpu.make_async_remote_copy(
            src_ref=src,
            dst_ref=dst,
            send_sem=send.at[half, stage, number],
            recv_sem=recv.at[half, stage, number],
            device_id={axis: wrap(places[half][stage] + step)},
            device_id_type=MESH,
        )

    low, high = pl.ds(0, 2), pl.ds(2, 2)
    first_copies = []
    for half in range(2):
        me = places[half][0]
        there, after, before = wrap(me + 2), wrap(me + 1), wrap(me - 1)
        batch = [
            copy(0, half, 0, 1, piece(half, there, low), relay.at[half, 0]),
            copy(1, half, 0, -1, piece(half, there, high), relay.at[half, 1]),
            copy(2, half, 0, 1, piece(half, after, high), message.at[half, 0, high]),
            copy(3, half, 0, -1, piece(half, before, low), message.at[half, 1, low]),
        ]
        first_copies.append(batch)
    for number in range(4):
        for half in range(2):
            first_copies[half][number].start()

    for half in range(2):
        me = places[half][0]
        for side, step, offset in ((0, 1, 0), (1, -1, 2)):
            first_copies[half][side].wait_recv()

            def add_relay(index, carry, half=half, side=side, step=step, offset=offset, me=me):
                second, block = lax.div(index, OWN), lax.rem(index, OWN)
                own = piece(half, wrap(me + step), second + offset)[block]
                got = relay[half, side, second, block]
                forward[half, side, second, block] = (own.astype(jnp.float32) + got.astype(jnp.float32)).astype(
                    jnp.bfloat16
                )
                return carry

            lax.fori_loop(0, 2 * OWN, add_relay, 0)
            last = copy(4 + side, half, 0, step, forward.at[half, side], message.at[half, side, pl.ds(offset, 2)])
            last.start()
            first_copies[half].append(last)

    second_copies = [[], []]
    for half in range(2):
        for number in range(2, 6):
            first_copies[half][number].wait_recv()
        me, other = places[half]

        def add_first(index, carry, half=half, me=me):
            second, block = lax.div(index, OWN), lax.rem(index, OWN)
            value = piece(half, me, second)[block].astype(jnp.float32)
            value += message[half, 0, second, block].astype(jnp.float32)
            value += message[half, 1, second, block].astype(jnp.float32)
            reduced[half, second, block] = value.astype(jnp.bfloat16)
            return carry

        lax.fori_loop(0, 4 * OWN, add_first, 0)
        there, after, before = wrap(other + 2), wrap(other + 1), wrap(other - 1)
        low3, high3 = pl.ds(0, 3), pl.ds(3, 3)
        batch = [
            copy(0, half, 1, 1, reduced.at[half, there, low3], relay2.at[half, 0]),
            copy(1, half, 1, -1, reduced.at[half, there, high3], relay2.at[half, 1]),
            copy(2, half, 1, 1, reduced.at[half, after, high3], message2.at[half, 0, high3]),
            copy(3, half, 1, -1, reduced.at[half, before, low3], message2.at[half, 1, low3]),
        ]
        for item in batch:
            item.start()
        second_copies[half] = batch

    for half in range(2):
        other = places[half][1]
        for side, step, offset in ((0, 1, 0), (1, -1, 3)):
            second_copies[half][side].wait_recv()
            target = wrap(other + step)
            for block in range(3):
                own = reduced[half, target, block + offset].astype(jnp.float32)
                got = relay2[half, side, block].astype(jnp.float32)
                forward2[half, side, block] = (own + got).astype(jnp.bfloat16)
            last = copy(4 + side, half, 1, step, forward2.at[half, side], message2.at[half, side, pl.ds(offset, 3)])
            last.start()
            second_copies[half].append(last)

    for half in range(2):
        other = places[half][1]
        for number in range(2, 6):
            second_copies[half][number].wait_recv()
        for block in range(OWN):
            value = reduced[half, other, block].astype(jnp.float32)
            value += message2[half, 0, block].astype(jnp.float32)
            value += message2[half, 1, block].astype(jnp.float32)
            out[block * BLOCK : (block + 1) * BLOCK, half * 128 : half * 128 + 128] = value.T

    for half in range(2):
        for item in first_copies[half] + second_copies[half]:
            item.wait_send()


def owner_sums(sums):
    vmem = pl.BlockSpec(memory_space=pltpu.VMEM)
    tile = (WIN // 2, BLOCK)
    return pl.pallas_call(
        reduce_kernel,
        out_shape=jax.ShapeDtypeStruct((OWN * BLOCK, WIN), jnp.float32),
        in_specs=[vmem],
        out_specs=vmem,
        scratch_shapes=[
            pltpu.VMEM((2, 2, 2, OWN, *tile), jnp.bfloat16),
            pltpu.VMEM((2, 2, 4, OWN, *tile), jnp.bfloat16),
            pltpu.VMEM((2, 2, 2, OWN, *tile), jnp.bfloat16),
            pltpu.VMEM((2, 4, OWN, *tile), jnp.bfloat16),
            pltpu.VMEM((2, 2, 3, *tile), jnp.bfloat16),
            pltpu.VMEM((2, 2, OWN, *tile), jnp.bfloat16),
            pltpu.VMEM((2, 2, 3, *tile), jnp.bfloat16),
            pltpu.SemaphoreType.DMA((2, 2, 6)),
            pltpu.SemaphoreType.DMA((2, 2, 6)),
        ],
        compiler_params=pltpu.CompilerParams(
            collective_id=1, has_side_effects=True, vmem_limit_bytes=40 * 1024 * 1024
        ),
    )(sums)


def directions(angles):
    u, v = angles[..., 0], angles[..., 1]
    return jnp.stack([jnp.cos(u) * jnp.cos(v), jnp.sin(u) * jnp.cos(v), jnp.sin(v)], -1)


def body(
    surface_data,
    panel_pos,
    panel_normal,
    panel_area,
    obs_pos,
    obs_angles,
    send_list,
    entry_source,
    entry_offset,
):
    z, y = lax.axis_index("z"), lax.axis_index("y")
    core, ax = lax.axis_index("core"), lax.axis_index("ax")
    line = z * NY + y

    surface = surface_data.reshape(AZL, AXL, 2 * BUF)
    edges = jnp.stack([surface[:, 0], surface[:, AXL - 1]], 0)
    geometry = jnp.concatenate(
        [panel_pos, panel_normal, panel_area[None], jnp.zeros_like(panel_area)[None]], 0
    ).reshape(8, BLOCKS_HERE, BLOCK).transpose(1, 0, 2)
    small = jnp.concatenate([geometry.reshape(-1), send_list.astype(jnp.bfloat16).reshape(-1)])
    small = jnp.pad(small, (0, 32 * 256 - small.shape[0])).reshape(32, 256)
    signals, asked = gather(
        surface, edges, small, obs_pos, directions(obs_angles.T).T, entry_source, entry_offset
    )
    pos = asked[:, : 3 * OWN].reshape(LINES, 3, OWN, BLOCK)
    dirs = asked[:, 40:43, :OWN].transpose(0, 2, 1)
    sources = asked[:, 24 : 24 + OWN, :32].astype(jnp.int32).reshape(ROWS, 32)
    offsets = asked[:, 32 : 32 + OWN, :32].astype(jnp.int32).reshape(ROWS, 32)
    toward = jnp.sum(dirs.transpose(0, 2, 1)[..., None] * pos, axis=1).reshape(ROWS, BLOCK)
    small = signals[:, BLOCKS_HERE * BUF :].reshape(GROUP, -1)
    geometry = small[:, : BLOCKS_HERE * 8 * BLOCK].reshape(SLOTS, 8, BLOCK).astype(jnp.float32)
    listed = small[:, BLOCKS_HERE * 8 * BLOCK : BLOCKS_HERE * 8 * BLOCK + 128].astype(jnp.int32)
    table = listed.reshape(GROUP, LINES, NC, NX)
    table = lax.dynamic_slice(table, (0, 0, core, ax), (GROUP, LINES, 1, 1)).reshape(GROUP, LINES)

    packed, counts = entry_codes(sources, offsets, table, line)
    sums = partial_sums(packed.reshape(-1), counts, dirs.reshape(-1), toward, geometry, signals)

    return owner_sums(sums.reshape(2, NZ, NY, OWN, WIN // 2, BLOCK))


def solution(mesh):
    split = Mesh(mesh.devices.reshape(NZ, NY, NC, NX), ("z", "y", "core", "ax"))
    azi, every = AZI, AZI + ("ax",)
    in_specs = (
        P(azi, "ax", None, None),
        P(None, azi, "ax"),
        P(None, azi, "ax"),
        P(azi, "ax"),
        P(None, every),
        P(None, every),
        P(every, None),
        P(every, None),
        P(every, None),
    )
    return jax.shard_map(body, mesh=split, in_specs=in_specs, out_specs=P(every, None), check_vma=False)
```
